32 devices in a mesh: groups: 2 (over y), expert: 4 (over z), replica: 4 (over x, core).
Axes of the slice: x: 2, y: 2, z: 4, core: 2. Of those that a mesh axis runs over, the one named last changes fastest.
Arguments:
- features: bfloat16 [65536, 256], P(('groups', 'expert', 'replica')), parts along dimension 0, may hold values from -6 to 6
- cotangents: bfloat16 [65536, 256], P(('groups', 'expert', 'replica')), parts along dimension 0, may hold values from -6 to 6
- routes: int32 [65536, 1], P(('groups', 'expert', 'replica')), parts along dimension 0, may hold values from 0 to 3; in each aligned block of 2048 rows (0 to 2047, 2048 to 4095, ...) at most 1024 rows name the same one
- live_counts: int32 [32], P(('groups', 'expert', 'replica')), parts along dimension 0, may hold values from 128 to 2048, as said below
- weights: float32 [8, 4, 256, 256], P(('groups', 'expert')), parts along dimension 0, may hold values from -0.5 to 0.5
- biases: float32 [8, 4, 256], P(('groups', 'expert')), parts along dimension 0, may hold values from -1.8 to 1.8
- first_moment: float32 [8, 4, 256, 256], P(('groups', 'expert'), None, 'replica'), parts along dimension 0, may hold values from -3 to 3
- second_moment: float32 [8, 4, 256, 256], P(('groups', 'expert'), None, 'replica'), parts along dimension 0, may hold values from 0.05 to 1
- bias_first: float32 [8, 4, 256], P(('groups', 'expert'), None, 'replica'), parts along dimension 0, may hold values from -3 to 3
- bias_second: float32 [8, 4, 256], P(('groups', 'expert'), None, 'replica'), parts along dimension 0, may hold values from 0.05 to 1
Outputs:
- input_grads: bfloat16 [65536, 256], P(('groups', 'expert', 'replica')), parts along dimension 0
- new_weights: float32 [8, 4, 256, 256], P(('groups', 'expert'), None, 'replica'), parts along dimension 0
- new_first: float32 [8, 4, 256, 256], P(('groups', 'expert'), None, 'replica'), parts along dimension 0
- new_second: float32 [8, 4, 256, 256], P(('groups', 'expert'), None, 'replica'), parts along dimension 0
- new_biases: float32 [8, 4, 256], P(('groups', 'expert'), None, 'replica'), parts along dimension 0
- new_bias_first: float32 [8, 4, 256], P(('groups', 'expert'), None, 'replica'), parts along dimension 0
- new_bias_second: float32 [8, 4, 256], P(('groups', 'expert'), None, 'replica'), parts along dimension 0
The draws below stay inside these ranges and needn't reach their ends.
There are 2 independent parts, one for each index of `groups`. The reference program is written for one: setup_inputs(seed, part) draws one part's arguments, and reference() takes and returns one part's arrays. A program takes and returns all parts, laid end to end along the dimension named above; each array names one. Nothing has to cross between parts.
Inputs may be any that keep to these rules, and one draw needn't show every extreme that they name: `routes`: among the 2048 rows of one device no expert is named more than 1024 times. `live_counts`: A multiple of 128; some device has all 2048 rows live.
All inputs are finite; a program needn't handle non-finite values.
Results may differ from the reference program's by a relative error of at most 0.0097.
Values may be sent and summed in bfloat16 or wider, within the bound.
A program may use at most 128 MiB of HBM per device.

```python
import math
import jax
import jax.numpy as jnp
import numpy as np
from jax import lax

W = 256
LAYERS = 4
ROWS_DEV = 2048
EXPERTS = 4
CAP = 1024
BLOCK = 128
DEVS = 16
RAYS = 32768
N_EXPERT = 4
N_REPLICA = 4


def draw_live_counts(key, part):
    key = jax.random.fold_in(key, 11)
    key_blocks, key_fullest = jax.random.split(key)
    blocks = jax.random.randint(key_blocks, (DEVS,), 1, ROWS_DEV // BLOCK + 1)
    fullest = jax.random.randint(key_fullest, (), 0, DEVS)
    counts = jnp.where(jnp.arange(DEVS) == fullest, ROWS_DEV // BLOCK, blocks)
    return (counts * BLOCK).astype(jnp.int32)


def level_of(rng, extent, shards, smallest, high):
    def one(dim, parts):
        steps = jax.random.uniform(jax.random.fold_in(jax.random.fold_in(rng, 6), dim), (parts,), jnp.float32, smallest / len(shards), high / len(shards))
        return jnp.repeat(jnp.exp(steps), extent[dim] // parts).reshape((-1,) + (1,) * (len(extent) - dim - 1))

    loudness = one(*shards[0])
    for cut in shards[1:]:
        loudness = loudness * one(*cut)
    return loudness


def shared_out(rng, own, number, rows, number_of, top, bound, lean):
    order = jax.random.permutation(rng, number_of)
    packed, common = portions_of(number_of, rows * top, bound, lean, True), portions_of(number_of, rows * top, bound, lean, False)
    places = jnp.arange(number_of)

    def named(tallies, rotation):
        used = int((tallies > 0).sum())
        fixed = max(1, used // 4)
        shifted = fixed + (places - fixed + rotation * (used - fixed)) % max(1, number_of - fixed)
        return jnp.zeros((number_of,), jnp.int32).at[order[jnp.where(places < fixed, places, shifted)]].set(jnp.asarray(tallies, jnp.int32))

    tallies = jnp.where(number % 4 == 0, named(packed, number // 4), named(common, number - number // 4 - 1))
    mixed = jax.random.permutation(jax.random.fold_in(own, 3), number_of)
    donor, sink = mixed[0:number_of // 2 * 2:2], mixed[1:number_of // 2 * 2:2]
    margin = jnp.minimum(tallies[donor] - 1, bound - tallies[sink]) // 2
    margin = jnp.where((donor == order[0]) | (sink == order[0]) | (tallies[sink] == 0), 0, jnp.maximum(margin, 0))
    shifted = jax.random.randint(jax.random.fold_in(own, 4), (number_of // 2,), 0, 1 << 20) % (margin + 1)
    tallies = tallies.at[donor].add(-shifted).at[sink].add(shifted)
    labels = jnp.searchsorted(jnp.cumsum(tallies), jnp.arange(rows * top), side="right").astype(jnp.int32)
    table = labels.reshape(top, rows).T
    table = table[jax.random.permutation(jax.random.fold_in(own, 1), rows)]
    rotation = jax.random.randint(jax.random.fold_in(own, 2), (rows, 1), 0, top)
    return jnp.take_along_axis(table, (jnp.arange(top)[None, :] + rotation) % top, axis=1)


def portions_of(amount, total, most, lean, full):
    loads = [(1 << 20) // math.isqrt(rank ** lean) + 1 for rank in range(1, amount + 1)]
    largest = most if full else min(most, max(-(-total // amount), total * loads[0] // sum(loads)))
    least = 1 if total - largest >= amount - 1 else 0
    holding, rest = [largest] + [least] * (amount - 1), total - largest - least * (amount - 1)
    while rest > 0:
        candidates = [i for i in range(1, amount) if holding[i] < largest] or [i for i in range(1, amount) if holding[i] < most]
        whole, left = sum([loads[i] for i in candidates]), rest
        for i in candidates:
            extra = min(most - holding[i], max(1, left * loads[i] // whole), rest)
            holding[i] = holding[i] + extra
            rest = rest - extra
    return np.array(holding)


def noise(stream_key, dims, deviation, limit, cuts=(), kind=jnp.bfloat16):
    loudness = level_of(stream_key, dims, cuts, -0.22, 0.18) if cuts else 1.0
    result = jax.random.normal(stream_key, dims, jnp.float32) * deviation * loudness
    return jnp.minimum(jnp.maximum(result, -limit), limit).astype(kind)


def setup_inputs(seed: int = 0, part: int = 0) -> dict:
    key_of = jax.random.split(jax.random.key(seed), 11)
    own_keys = jax.random.split(jax.random.fold_in(key_of[10], part), 11)
    features = noise(own_keys[0], (RAYS, W), 1.0, 6.0, ((0, 16),))
    cotangents = noise(own_keys[1], (RAYS, W), 1.0, 6.0, ((0, 16),))
    routes_keys = jax.random.split(jax.random.fold_in(own_keys[2], 1), RAYS // ROWS_DEV)
    routes_turns = jax.random.permutation(jax.random.fold_in(own_keys[2], 3), RAYS // ROWS_DEV)
    routes = jax.vmap(lambda own, number: shared_out(jax.random.fold_in(own_keys[2], 2), own, number, ROWS_DEV, EXPERTS, 1, CAP, 2))(routes_keys, routes_turns).reshape((RAYS, 1))
    live_counts = draw_live_counts(jax.random.fold_in(jax.random.fold_in(key_of[10], part), 71), part)
    weights = noise(own_keys[4], (EXPERTS, LAYERS, W, W), (W // 2) ** -0.5, 0.5, ((0, 4),), jnp.float32)
    biases = noise(own_keys[5], (EXPERTS, LAYERS, W), 0.3, 1.8, ((0, 4),), jnp.float32)
    first_moment = noise(own_keys[6], (EXPERTS, LAYERS, W, W), 0.5, 3.0, ((0, 4), (2, 4)), jnp.float32)
    second_moment = jnp.clip(jnp.exp(math.log(1.0) - 2.9957323 * jax.random.uniform(own_keys[7], (EXPERTS, LAYERS, W, W), jnp.float32) ** level_of(own_keys[7], (EXPERTS, LAYERS, W, W), ((0, 4), (2, 4)), -0.2, 0.2)), 0.05, 1.0)
    bias_first = noise(own_keys[8], (EXPERTS, LAYERS, W), 0.5, 3.0, ((0, 4), (2, 4)), jnp.float32)
    bias_second = jnp.clip(jnp.exp(math.log(1.0) - 2.9957323 * jax.random.uniform(own_keys[9], (EXPERTS, LAYERS, W), jnp.float32) ** level_of(own_keys[9], (EXPERTS, LAYERS, W), ((0, 4), (2, 4)), -0.2, 0.2)), 0.05, 1.0)
    return {"features": features, "cotangents": cotangents, "routes": routes, "live_counts": live_counts, "weights": weights, "biases": biases, "first_moment": first_moment, "second_moment": second_moment, "bias_first": bias_first, "bias_second": bias_second}


beta_first = 0.9
beta_second = 0.999
learn_rate = 0.05
adam_epsilon = 1e-08
first_fix = 1.0 - 0.9 ** 10
second_fix = 1.0 - 0.999 ** 10

def expert_backward(weights_low, bias_rows, inputs_rows, adjoint):
    activations = [inputs_rows]
    preacts = []
    for layer in range(LAYERS - 1):
        preact = jnp.dot(activations[-1], weights_low[layer], preferred_element_type=jnp.float32) + bias_rows[layer]
        preacts.append(preact)
        activations.append(jax.nn.softplus(preact).astype(jnp.bfloat16))
    weight_grads = [None] * LAYERS
    bias_grads = [None] * LAYERS
    input_grad = None
    for layer in reversed(range(LAYERS)):
        weight_grads[layer] = lax.dot_general(activations[layer], adjoint, (((0,), (0,)), ((), ())), preferred_element_type=jnp.float32)
        bias_grads[layer] = lax.optimization_barrier(jnp.sum(adjoint.astype(jnp.float32), 0))
        pulled = lax.dot_general(adjoint, weights_low[layer], (((1,), (1,)), ((), ())), preferred_element_type=jnp.float32)
        if layer > 0:
            adjoint = (pulled * jax.nn.sigmoid(preacts[layer - 1])).astype(jnp.bfloat16)
        else:
            input_grad = pulled.astype(jnp.bfloat16)
    return (input_grad, jnp.stack(weight_grads), jnp.stack(bias_grads))

def adam_update(master, moment_one, moment_two, gradient):
    scaled = gradient / math.sqrt(ROWS_DEV)
    moment_one = beta_first * moment_one + (1.0 - beta_first) * scaled
    moment_two = beta_second * moment_two + (1.0 - beta_second) * scaled * scaled
    updated = master - learn_rate * (moment_one / first_fix) / (jnp.sqrt(moment_two / second_fix) + adam_epsilon)
    return (updated, moment_one, moment_two)

def reference(features, cotangents, routes, live_counts, weights, biases, first_moment, second_moment, bias_first, bias_second):
    route_ids = routes[:, 0]
    ray_index = jnp.arange(RAYS, dtype=jnp.int32)
    device = ray_index // ROWS_DEV
    is_live = ray_index % ROWS_DEV < live_counts[device]
    masked = jnp.where(is_live[:, None], cotangents, jnp.zeros_like(cotangents))
    most_rows = CAP * N_EXPERT * N_REPLICA
    feature_pad = jnp.concatenate([features, jnp.zeros((1, W), features.dtype)], 0)
    adjoint_pad = jnp.concatenate([masked, jnp.zeros((1, W), masked.dtype)], 0)

    def per_expert(total, expert):
        picked = jnp.nonzero(route_ids == expert, size=most_rows, fill_value=RAYS)[0].astype(jnp.int32)
        weights_low = weights[expert].astype(jnp.bfloat16)
        input_grad, weight_grads, bias_grads = expert_backward(weights_low, biases[expert], feature_pad[picked], adjoint_pad[picked])
        total = total.at[picked].set(input_grad, mode='drop')
        return (total, (weight_grads, bias_grads))
    input_grads, (weight_grads, bias_grads) = lax.scan(per_expert, jnp.zeros((RAYS, W), jnp.bfloat16), jnp.arange(EXPERTS, dtype=jnp.int32))
    new_weights, new_first, new_second = adam_update(weights, first_moment, second_moment, weight_grads)
    new_biases, new_bias_first, new_bias_second = adam_update(biases, bias_first, bias_second, bias_grads)
    return (input_grads, new_weights, new_first, new_second, new_biases, new_bias_first, new_bias_second)
```

```python
import functools
import math

import jax
import jax.numpy as jnp
from jax import lax
from jax.experimental import pallas as pl
from jax.experimental.pallas import tpu as pltpu
from jax.sharding import PartitionSpec as P

LAYERS = 4
ROWS_DEV = 2048


beta_first = 0.9
beta_second = 0.999
learn_rate = 0.05
adam_epsilon = 1e-08
first_fix = 1.0 - 0.9**10
second_fix = 1.0 - 0.999**10


def forward_layers(weights_low, bias_rows, inputs_rows):
    activations = [inputs_rows]
    preacts = []
    for layer in range(LAYERS - 1):
        preact = (
            jnp.dot(activations[-1], weights_low[layer], preferred_element_type=jnp.float32)
            + bias_rows[layer]
        )
        preacts.append(preact)
        activations.append(jax.nn.softplus(preact).astype(jnp.bfloat16))
    return (activations, preacts)


def adjoint_chain(weights_low, preacts, adjoint):
    adjoints = [None] * LAYERS
    input_grad = None
    for layer in reversed(range(LAYERS)):
        adjoints[layer] = adjoint
        pulled = lax.dot_general(
            adjoint,
            weights_low[layer],
            (((1,), (1,)), ((), ())),
            preferred_element_type=jnp.float32,
        )
        if layer > 0:
            adjoint = (pulled * jax.nn.sigmoid(preacts[layer - 1])).astype(jnp.bfloat16)
        else:
            input_grad = pulled.astype(jnp.bfloat16)
    return (adjoints, input_grad)


def gradient_terms(activations, adjoints):
    weight_grads = []
    bias_grads = []
    for layer in range(LAYERS):
        weight_grads.append(
            lax.dot_general(
                activations[layer],
                adjoints[layer],
                (((0,), (0,)), ((), ())),
                preferred_element_type=jnp.float32,
            )
        )
        bias_grads.append(jnp.sum(adjoints[layer].astype(jnp.float32), 0))
    return (jnp.stack(weight_grads)[None], jnp.stack(bias_grads)[None])


def adam_update(master, moment_one, moment_two, gradient):
    scaled = gradient / math.sqrt(ROWS_DEV)
    moment_one = beta_first * moment_one + (1.0 - beta_first) * scaled
    moment_two = beta_second * moment_two + (1.0 - beta_second) * scaled * scaled
    updated = master - learn_rate * (moment_one / first_fix) / (
        jnp.sqrt(moment_two / second_fix) + adam_epsilon
    )
    return (updated, moment_one, moment_two)


def routed_shards(
    features,
    cotangents,
    routes,
    live_counts,
    weights,
    biases,
    first_moment,
    second_moment,
    bias_first,
    bias_second,
):
    expert_count = lax.axis_size("expert")
    replicas = lax.axis_size("replica")
    rows_here = features.shape[0]
    feature_width = features.shape[1]
    capacity = 2 * rows_here // expert_count
    route_ids = routes[:, 0]
    positions = lax.iota(jnp.int32, rows_here)
    is_live = positions < live_counts[0]
    masked = jnp.where(is_live[:, None], cotangents, jnp.zeros_like(cotangents))
    onehot = (route_ids[:, None] == lax.iota(jnp.int32, expert_count)[None, :]).astype(jnp.int32)
    weights_low = weights[0].astype(jnp.bfloat16)
    dump_slot = expert_count * capacity
    slot_rank = jnp.sum((jnp.cumsum(onehot, 0) - onehot) * onehot, 1)
    slot_index = route_ids * capacity + slot_rank

    def place(row_data):
        buffer = (
            jnp.zeros((expert_count * capacity, feature_width), row_data.dtype)
            .at[slot_index]
            .set(row_data, mode="drop")
        )
        return buffer.reshape(expert_count, capacity, feature_width)

    got_rows, got_adjoint = (
        lax.all_to_all(place(features), "expert", split_axis=0, concat_axis=0, tiled=True),
        lax.all_to_all(place(masked), "expert", split_axis=0, concat_axis=0, tiled=True),
    )
    inputs_rows = got_rows.reshape(-1, feature_width)
    adjoint = got_adjoint.reshape(-1, feature_width)
    activations, preacts = forward_layers(weights_low, biases[0], inputs_rows)
    adjoints, input_grad = adjoint_chain(weights_low, preacts, adjoint)
    weight_grads, bias_grads = gradient_terms(activations, adjoints)
    returned = lax.all_to_all(
        input_grad.reshape(expert_count, capacity, feature_width),
        "expert",
        split_axis=0,
        concat_axis=0,
        tiled=True,
    )
    flat = returned.reshape(-1, feature_width)
    picked = flat[jnp.minimum(slot_index, dump_slot - 1)]
    input_grads = jnp.where((slot_index < dump_slot)[:, None], picked, jnp.zeros_like(picked))
    shard_rows = feature_width // replicas
    shard_start = lax.axis_index("replica") * shard_rows
    weight_share, bias_share = (
        lax.psum_scatter(
            weight_grads.astype(jnp.bfloat16), "replica", scatter_dimension=2, tiled=True
        ).astype(jnp.float32),
        lax.psum_scatter(
            bias_grads.astype(jnp.bfloat16), "replica", scatter_dimension=2, tiled=True
        ).astype(jnp.float32),
    )
    master_weights = lax.dynamic_slice_in_dim(weights, shard_start, shard_rows, 2)
    master_biases = lax.dynamic_slice_in_dim(biases, shard_start, shard_rows, 2)
    new_weights, new_first, new_second = adam_update(
        master_weights, first_moment, second_moment, weight_share
    )
    new_biases, new_bias_first, new_bias_second = adam_update(
        master_biases, bias_first, bias_second, bias_share
    )
    return (
        input_grads,
        new_weights,
        new_first,
        new_second,
        new_biases,
        new_bias_first,
        new_bias_second,
    )


TILE = 512
SLICE = 64
TAIL = 16


def softplus_and_sigmoid(x):
    small = jnp.exp(-jnp.abs(x))
    total = 1.0 + small
    inverse = pl.reciprocal(total)
    log_part = jnp.where(small < 1e-3, small - 0.5 * small * small, jnp.log(total))
    return jnp.maximum(x, 0.0) + log_part, jnp.where(x >= 0.0, inverse, small * inverse)


def fused_kernel(
    experts,
    live_ref,
    features_ref,
    cotangents_ref,
    routes_ref,
    weights_ref,
    biases_ref,
    first_ref,
    second_ref,
    bias_first_ref,
    bias_second_ref,
    input_grads_ref,
    new_weights_ref,
    new_first_ref,
    new_second_ref,
    new_biases_ref,
    new_bias_first_ref,
    new_bias_second_ref,
    low,
    bias_all,
    onehot,
    mask,
    acts,
    sigs,
    adj,
    grad,
    bias_grad,
    core_send,
    core_recv,
    core_keep,
    chip_send,
    chip_recv,
    chip_keep,
    line_send,
    line_recv,
    z_sems,
    x_sems,
    c_sems,
    b_sems,
    core_sems,
    chip_sems,
    line_sems,
):
    rows, width = features_ref.shape
    wide = experts * width
    tiles = rows // TILE
    expert = lax.axis_index("expert")
    replica = lax.axis_index("replica")
    chip, core = replica // 2, replica % 2
    other_core = {"replica": chip * 2 + 1 - core}
    other_chip = {"replica": (1 - chip) * 2 + core}
    others = range(1, experts)

    def along(d):
        return {"expert": lax.rem(expert + d, experts)}

    def before(d):
        return lax.rem(expert + d, experts)

    barrier = pltpu.get_barrier_semaphore()
    for peer in [other_core, other_chip] + [along(d) for d in others]:
        pl.semaphore_signal(barrier, inc=1, device_id=peer, device_id_type=pl.DeviceIdType.MESH)
    for layer in range(LAYERS):
        low[layer, expert] = weights_ref[layer].astype(jnp.bfloat16)
    bias_all[expert] = jnp.concatenate([biases_ref[...], jnp.zeros_like(biases_ref)], 0)
    pl.semaphore_wait(barrier, experts + 1)

    started = []

    def send(src, dst, sems, index, peer):
        copy = pltpu.make_async_remote_copy(
            src_ref=src,
            dst_ref=dst,
            send_sem=sems.at[(0,) + index],
            recv_sem=sems.at[(1,) + index],
            device_id=peer,
            device_id_type=pl.DeviceIdType.MESH,
        )
        copy.start()
        started.append(copy)
        return copy

    own_start = pl.multiple_of(core * 2 * SLICE + chip * SLICE, SLICE)
    half_start = pl.multiple_of(core * 2 * SLICE, 2 * SLICE)
    bias_copies = []
    line_copies = []
    for layer in range(LAYERS):
        quarter = low.at[layer, expert, pl.ds(own_start, SLICE)]
        line_copies.append([send(quarter, quarter, z_sems, (layer, d - 1), along(d)) for d in others])
        if layer == 0:
            whole = bias_all.at[expert]
            bias_copies = [send(whole, whole, b_sems, (d - 1,), along(d)) for d in others]

    chip_copies = {}
    core_copies = {}

    def pass_to_chip(layer):
        chip_copies[layer] = []
        for copy in line_copies[layer]:
            copy.wait_recv()
        for d in others:
            part = low.at[layer, before(d), pl.ds(own_start, SLICE)]
            chip_copies[layer].append(send(part, part, x_sems, (layer, d - 1), other_chip))

    def pass_to_core(layer):
        core_copies[layer] = []
        for copy in chip_copies[layer]:
            copy.wait_recv()
        for d in others:
            part = low.at[layer, before(d), pl.ds(half_start, 2 * SLICE)]
            core_copies[layer].append(send(part, part, c_sems, (layer, d - 1), other_core))

    def arrived(layer):
        for copy in core_copies[layer]:
            copy.wait_recv()

    def each_tile(body):
        def step(i, carry):
            body(pl.ds(pl.multiple_of(i * TILE, TILE), TILE))
            return carry

        lax.fori_loop(0, tiles, step, 0)

    row_of = lax.broadcasted_iota(jnp.int32, (16, rows), 0)
    position = lax.broadcasted_iota(jnp.int32, (16, rows), 1)
    named = (routes_ref[...] == row_of % experts) & (row_of < 3 * experts)
    named = named & (position < live_ref[0])
    onehot[...] = jnp.where(named, 1.0, 0.0).astype(jnp.bfloat16)
    spread_row = lax.broadcasted_iota(jnp.int32, (16, wide), 0)
    spread_column = lax.broadcasted_iota(jnp.int32, (16, wide), 1)
    spread = jnp.where(spread_row == spread_column // width, 1.0, 0.0).astype(jnp.bfloat16)
    contract_rows = (((0,), (0,)), ((), ()))

    for copy in bias_copies:
        copy.wait_recv()
    bias_parts = []
    for layer in range(LAYERS - 1):
        whole = jnp.concatenate([bias_all[e, layer : layer + 1] for e in range(experts)], 0)
        high = whole.astype(jnp.bfloat16).astype(jnp.float32)
        middle = (whole - high).astype(jnp.bfloat16).astype(jnp.float32)
        lowest = whole - high - middle
        bias_parts.append(
            jnp.concatenate([high, middle, lowest, jnp.zeros_like(high)], 0).astype(jnp.bfloat16)
        )

    def prepare(at):
        chosen = onehot[:, at]
        mask[at, :] = lax.dot_general(
            chosen, spread, contract_rows, preferred_element_type=jnp.float32
        ).astype(jnp.bfloat16)
        for layer in range(LAYERS - 1):
            sigs[layer, at, :] = lax.dot_general(
                chosen, bias_parts[layer], contract_rows, preferred_element_type=jnp.float32
            )

    each_tile(prepare)

    def separated(block, at):
        return jnp.concatenate([block] * experts, 1) * mask[at, :]

    def forward(layer):
        def body(at):
            block = features_ref[at, :] if layer == 0 else acts[layer - 1, at, :]
            preact = (
                jnp.dot(
                    separated(block, at),
                    low[layer].reshape(wide, width),
                    preferred_element_type=jnp.float32,
                )
                + sigs[layer, at, :]
            )
            soft, sig = softplus_and_sigmoid(preact)
            acts[layer, at, :] = soft.astype(jnp.bfloat16)
            sigs[layer, at, :] = sig

        each_tile(body)

    pass_to_chip(0)
    pass_to_chip(1)
    pass_to_core(0)
    arrived(0)
    forward(0)
    pass_to_chip(2)
    pass_to_core(1)
    pass_to_chip(3)
    arrived(1)
    forward(1)
    pass_to_core(2)
    pass_to_core(3)
    arrived(2)
    forward(2)
    arrived(3)

    def adjoint_of(layer, at):
        return cotangents_ref[at, :] if layer == LAYERS - 1 else adj[at, :]

    def gradients(layer):
        grad[...] = jnp.zeros_like(grad)
        bias_grad[layer] = jnp.zeros((16, width), jnp.float32)

        def body(at):
            block = adjoint_of(layer, at)
            act = features_ref[at, :] if layer == 0 else acts[layer - 1, at, :]
            grad[...] += lax.dot_general(
                act, separated(block, at), contract_rows, preferred_element_type=jnp.float32
            )
            bias_grad[layer] += jnp.dot(onehot[:, at], block, preferred_element_type=jnp.float32)

        each_tile(body)

    def pull(layer):
        def body(at):
            parts = separated(adjoint_of(layer, at), at)
            pulled = sum(
                lax.dot_general(
                    parts[:, e * width : (e + 1) * width],
                    low[layer, e],
                    (((1,), (1,)), ((), ())),
                    preferred_element_type=jnp.float32,
                )
                for e in range(experts)
            )
            if layer > 0:
                adj[at, :] = (pulled * sigs[layer - 1, at, :]).astype(jnp.bfloat16)
            else:
                input_grads_ref[at, :] = pulled.astype(jnp.bfloat16)

        each_tile(body)

    def height(layer):
        return SLICE + (TAIL if layer == 0 else 0)

    sums = {}

    def share_core(layer):
        for e in range(experts):
            columns = slice(e * width, (e + 1) * width)
            if layer == 0:
                tail = jnp.concatenate(
                    [bias_grad[k, e : e + 1] for k in range(LAYERS)]
                    + [jnp.zeros((TAIL - LAYERS, width), jnp.float32)],
                    0,
                )
            for c in range(2):
                mine = pl.ds(pl.multiple_of((c * 2 + core) * SLICE, SLICE), SLICE)
                theirs = pl.ds(pl.multiple_of((c * 2 + 1 - core) * SLICE, SLICE), SLICE)
                core_keep[layer, c, e, :SLICE] = grad[mine, columns]
                core_send[layer, c, e, :SLICE] = grad[theirs, columns].astype(jnp.bfloat16)
                if layer == 0:
                    core_keep[layer, c, e, SLICE:] = tail
                    core_send[layer, c, e, SLICE:] = tail.astype(jnp.bfloat16)
        part = pl.ds(0, height(layer))
        sums["core", layer] = send(
            core_send.at[layer, :, :, part],
            core_recv.at[layer, :, :, part],
            core_sems,
            (layer,),
            other_core,
        )

    def share_chip(layer):
        sums["core", layer].wait_recv()
        n = height(layer)
        for e in range(experts):
            chip_send[layer, e, :n] = (
                core_keep[layer, 1 - chip, e, :n]
                + core_recv[layer, 1 - chip, e, :n].astype(jnp.float32)
            ).astype(jnp.bfloat16)
        part = pl.ds(0, n)
        sums["chip", layer] = send(
            chip_send.at[layer, :, part], chip_recv.at[layer, :, part], chip_sems, (layer,), other_chip
        )
        for e in range(experts):
            chip_keep[layer, e, :n] = core_keep[layer, chip, e, :n] + core_recv[
                layer, chip, e, :n
            ].astype(jnp.float32)

    def share_line(layer):
        sums["chip", layer].wait_recv()
        n = height(layer)
        for e in range(experts):
            total = chip_keep[layer, e, :n] + chip_recv[layer, e, :n].astype(jnp.float32)
            chip_keep[layer, e, :n] = total
            line_send[layer, e, :n] = total.astype(jnp.bfloat16)
        part = pl.ds(0, n)
        sums["line", layer] = [
            send(
                line_send.at[layer, before(d), part],
                line_recv.at[layer, d - 1, part],
                line_sems,
                (layer, d - 1),
                along(d),
            )
            for d in others
        ]

    def finish(layer):
        for copy in sums["line", layer]:
            copy.wait_recv()
        n = height(layer)
        total = chip_keep[layer, expert, :n]
        for d in others:
            total = total + line_recv[layer, d - 1, :n].astype(jnp.float32)
        master = weights_ref[layer, pl.ds(pl.multiple_of(replica * SLICE, SLICE), SLICE), :]
        updated, one, two = adam_update(master, first_ref[layer], second_ref[layer], total[:SLICE])
        new_weights_ref[layer] = updated
        new_first_ref[layer] = one
        new_second_ref[layer] = two
        if layer == 0:

            def own_columns(block):
                picked = block[:, :SLICE]
                for k in range(1, width // SLICE):
                    picked = jnp.where(replica == k, block[:, k * SLICE : (k + 1) * SLICE], picked)
                return picked

            updated, one, two = adam_update(
                own_columns(biases_ref[...]),
                bias_first_ref[...],
                bias_second_ref[...],
                own_columns(total[SLICE : SLICE + LAYERS]),
            )
            new_biases_ref[...] = updated
            new_bias_first_ref[...] = one
            new_bias_second_ref[...] = two

    gradients(3)
    share_core(3)
    pull(3)
    share_chip(3)
    gradients(2)
    share_core(2)
    share_line(3)
    pull(2)
    share_chip(2)
    gradients(1)
    share_core(1)
    share_line(2)
    pull(1)
    share_chip(1)
    gradients(0)
    share_core(0)
    share_line(1)
    pull(0)
    share_chip(0)
    finish(3)
    finish(2)
    share_line(0)
    finish(1)
    finish(0)
    for copy in started:
        copy.wait_send()


def fused_shards(
    features,
    cotangents,
    routes,
    live_counts,
    weights,
    biases,
    first_moment,
    second_moment,
    bias_first,
    bias_second,
):
    experts = lax.axis_size("expert")
    rows, width = features.shape
    wide = experts * width
    tall = SLICE + TAIL
    f32, bf16 = jnp.float32, jnp.bfloat16
    vmem = pl.BlockSpec(memory_space=pltpu.VMEM)
    moment = jax.ShapeDtypeStruct(first_moment.shape[1:], f32)
    bias_moment = jax.ShapeDtypeStruct(bias_first.shape[1:], f32)
    outs = pl.pallas_call(
        functools.partial(fused_kernel, experts),
        out_shape=(
            jax.ShapeDtypeStruct((rows, width), bf16),
            moment,
            moment,
            moment,
            bias_moment,
            bias_moment,
            bias_moment,
        ),
        in_specs=[pl.BlockSpec(memory_space=pltpu.SMEM)] + [vmem] * 9,
        out_specs=(vmem,) * 7,
        scratch_shapes=[
            pltpu.VMEM((LAYERS, experts, width, width), bf16),
            pltpu.VMEM((experts, 2 * LAYERS, width), f32),
            pltpu.VMEM((16, rows), bf16),
            pltpu.VMEM((rows, wide), bf16),
            pltpu.VMEM((LAYERS - 1, rows, width), bf16),
            pltpu.VMEM((LAYERS - 1, rows, width), f32),
            pltpu.VMEM((rows, width), bf16),
            pltpu.VMEM((width, wide), f32),
            pltpu.VMEM((LAYERS, 16, width), f32),
            pltpu.VMEM((LAYERS, 2, experts, tall, width), bf16),
            pltpu.VMEM((LAYERS, 2, experts, tall, width), bf16),
            pltpu.VMEM((LAYERS, 2, experts, tall, width), f32),
            pltpu.VMEM((LAYERS, experts, tall, width), bf16),
            pltpu.VMEM((LAYERS, experts, tall, width), bf16),
            pltpu.VMEM((LAYERS, experts, tall, width), f32),
            pltpu.VMEM((LAYERS, experts, tall, width), bf16),
            pltpu.VMEM((LAYERS, experts - 1, tall, width), bf16),
            pltpu.SemaphoreType.DMA((2, LAYERS, experts - 1)),
            pltpu.SemaphoreType.DMA((2, LAYERS, experts - 1)),
            pltpu.SemaphoreType.DMA((2, LAYERS, experts - 1)),
            pltpu.SemaphoreType.DMA((2, experts - 1)),
            pltpu.SemaphoreType.DMA((2, LAYERS)),
            pltpu.SemaphoreType.DMA((2, LAYERS)),
            pltpu.SemaphoreType.DMA((2, LAYERS, experts - 1)),
        ],
        compiler_params=pltpu.CompilerParams(
            collective_id=0, has_side_effects=True, vmem_limit_bytes=56 * 1024 * 1024
        ),
        cost_estimate=pl.CostEstimate(
            flops=22 * rows * wide * width, bytes_accessed=6 * 2**20, transcendentals=9 * rows * width
        ),
    )(
        live_counts,
        features,
        cotangents,
        routes.reshape(1, rows),
        weights[0],
        biases[0],
        first_moment[0],
        second_moment[0],
        bias_first[0],
        bias_second[0],
    )
    return (outs[0],) + tuple(out[None] for out in outs[1:])


def shards(*arrays):
    if lax.axis_size("expert") == 4 and lax.axis_size("replica") == 4:
        return fused_shards(*arrays)
    return routed_shards(*arrays)


def solution(mesh):
    return jax.shard_map(
        shards,
        mesh=mesh,
        in_specs=(
            P(("groups", "expert", "replica"), None),
            P(("groups", "expert", "replica"), None),
            P(("groups", "expert", "replica"), None),
            P(("groups", "expert", "replica")),
            P(("groups", "expert"), None, None, None),
            P(("groups", "expert"), None, None),
            P(("groups", "expert"), None, "replica", None),
            P(("groups", "expert"), None, "replica", None),
            P(("groups", "expert"), None, "replica"),
            P(("groups", "expert"), None, "replica"),
        ),
        out_specs=(
            P(("groups", "expert", "replica"), None),
            P(("groups", "expert"), None, "replica", None),
            P(("groups", "expert"), None, "replica", None),
            P(("groups", "expert"), None, "replica", None),
            P(("groups", "expert"), None, "replica"),
            P(("groups", "expert"), None, "replica"),
            P(("groups", "expert"), None, "replica"),
        ),
        check_vma=False,
    )
```

```python
import functools
import math

import jax
import jax.numpy as jnp
from jax import lax
from jax.experimental import pallas as pl
from jax.experimental.pallas import tpu as pltpu
from jax.sharding import PartitionSpec as P

LAYERS = 4
ROWS_DEV = 2048


beta_first = 0.9
beta_second = 0.999
learn_rate = 0.05
adam_epsilon = 1e-08
first_fix = 1.0 - 0.9**10
second_fix = 1.0 - 0.999**10


def forward_layers(weights_low, bias_rows, inputs_rows):
    activations = [inputs_rows]
    preacts = []
    for layer in range(LAYERS - 1):
        preact = (
            jnp.dot(activations[-1], weights_low[layer], preferred_element_type=jnp.float32)
            + bias_rows[layer]
        )
        preacts.append(preact)
        activations.append(jax.nn.softplus(preact).astype(jnp.bfloat16))
    return (activations, preacts)


def adjoint_chain(weights_low, preacts, adjoint):
    adjoints = [None] * LAYERS
    input_grad = None
    for layer in reversed(range(LAYERS)):
        adjoints[layer] = adjoint
        pulled = lax.dot_general(
            adjoint,
            weights_low[layer],
            (((1,), (1,)), ((), ())),
            preferred_element_type=jnp.float32,
        )
        if layer > 0:
            adjoint = (pulled * jax.nn.sigmoid(preacts[layer - 1])).astype(jnp.bfloat16)
        else:
            input_grad = pulled.astype(jnp.bfloat16)
    return (adjoints, input_grad)


def gradient_terms(activations, adjoints):
    weight_grads = []
    bias_grads = []
    for layer in range(LAYERS):
        weight_grads.append(
            lax.dot_general(
                activations[layer],
                adjoints[layer],
                (((0,), (0,)), ((), ())),
                preferred_element_type=jnp.float32,
            )
        )
        bias_grads.append(jnp.sum(adjoints[layer].astype(jnp.float32), 0))
    return (jnp.stack(weight_grads)[None], jnp.stack(bias_grads)[None])


def adam_update(master, moment_one, moment_two, gradient):
    scaled = gradient / math.sqrt(ROWS_DEV)
    moment_one = beta_first * moment_one + (1.0 - beta_first) * scaled
    moment_two = beta_second * moment_two + (1.0 - beta_second) * scaled * scaled
    updated = master - learn_rate * (moment_one / first_fix) / (
        jnp.sqrt(moment_two / second_fix) + adam_epsilon
    )
    return (updated, moment_one, moment_two)


def routed_shards(
    features,
    cotangents,
    routes,
    live_counts,
    weights,
    biases,
    first_moment,
    second_moment,
    bias_first,
    bias_second,
):
    expert_count = lax.axis_size("expert")
    replicas = lax.axis_size("replica")
    rows_here = features.shape[0]
    feature_width = features.shape[1]
    capacity = 2 * rows_here // expert_count
    route_ids = routes[:, 0]
    positions = lax.iota(jnp.int32, rows_here)
    is_live = positions < live_counts[0]
    masked = jnp.where(is_live[:, None], cotangents, jnp.zeros_like(cotangents))
    onehot = (route_ids[:, None] == lax.iota(jnp.int32, expert_count)[None, :]).astype(jnp.int32)
    weights_low = weights[0].astype(jnp.bfloat16)
    dump_slot = expert_count * capacity
    slot_rank = jnp.sum((jnp.cumsum(onehot, 0) - onehot) * onehot, 1)
    slot_index = route_ids * capacity + slot_rank

    def place(row_data):
        buffer = (
            jnp.zeros((expert_count * capacity, feature_width), row_data.dtype)
            .at[slot_index]
            .set(row_data, mode="drop")
        )
        return buffer.reshape(expert_count, capacity, feature_width)

    got_rows, got_adjoint = (
        lax.all_to_all(place(features), "expert", split_axis=0, concat_axis=0, tiled=True),
        lax.all_to_all(place(masked), "expert", split_axis=0, concat_axis=0, tiled=True),
    )
    inputs_rows = got_rows.reshape(-1, feature_width)
    adjoint = got_adjoint.reshape(-1, feature_width)
    activations, preacts = forward_layers(weights_low, biases[0], inputs_rows)
    adjoints, input_grad = adjoint_chain(weights_low, preacts, adjoint)
    weight_grads, bias_grads = gradient_terms(activations, adjoints)
    returned = lax.all_to_all(
        input_grad.reshape(expert_count, capacity, feature_width),
        "expert",
        split_axis=0,
        concat_axis=0,
        tiled=True,
    )
    flat = returned.reshape(-1, feature_width)
    picked = flat[jnp.minimum(slot_index, dump_slot - 1)]
    input_grads = jnp.where((slot_index < dump_slot)[:, None], picked, jnp.zeros_like(picked))
    shard_rows = feature_width // replicas
    shard_start = lax.axis_index("replica") * shard_rows
    weight_share, bias_share = (
        lax.psum_scatter(
            weight_grads.astype(jnp.bfloat16), "replica", scatter_dimension=2, tiled=True
        ).astype(jnp.float32),
        lax.psum_scatter(
            bias_grads.astype(jnp.bfloat16), "replica", scatter_dimension=2, tiled=True
        ).astype(jnp.float32),
    )
    master_weights = lax.dynamic_slice_in_dim(weights, shard_start, shard_rows, 2)
    master_biases = lax.dynamic_slice_in_dim(biases, shard_start, shard_rows, 2)
    new_weights, new_first, new_second = adam_update(
        master_weights, first_moment, second_moment, weight_share
    )
    new_biases, new_bias_first, new_bias_second = adam_update(
        master_biases, bias_first, bias_second, bias_share
    )
    return (
        input_grads,
        new_weights,
        new_first,
        new_second,
        new_biases,
        new_bias_first,
        new_bias_second,
    )


TILE = 1024
SLICE = 64
TAIL = 16


def softplus_and_sigmoid(x):
    small = jnp.exp(-jnp.abs(x))
    total = 1.0 + small
    inverse = pl.reciprocal(total)
    log_part = jnp.where(small < 1e-3, small - 0.5 * small * small, jnp.log(total))
    return jnp.maximum(x, 0.0) + log_part, jnp.where(x >= 0.0, inverse, small * inverse)


def fused_kernel(
    experts,
    live_ref,
    features_hbm,
    cotangents_hbm,
    routes_ref,
    weights_hbm,
    biases_ref,
    input_grads_ref,
    share_ref,
    bias_share_ref,
    master,
    features_ref,
    cotangents_ref,
    low,
    bias_all,
    onehot,
    mask,
    acts,
    sigs,
    adj,
    grad,
    bias_grad,
    core_send,
    core_recv,
    core_keep,
    chip_send,
    chip_recv,
    chip_keep,
    line_send,
    line_recv,
    z_sems,
    x_sems,
    c_sems,
    b_sems,
    core_sems,
    chip_sems,
    line_sems,
    load_sems,
):
    rows, width = features_ref.shape
    wide = experts * width
    tiles = rows // TILE
    expert = lax.axis_index("expert")
    replica = lax.axis_index("replica")
    chip, core = replica // 2, replica % 2
    other_core = {"replica": chip * 2 + 1 - core}
    other_chip = {"replica": (1 - chip) * 2 + core}
    others = range(1, experts)

    def along(d):
        return {"expert": lax.rem(expert + d, experts)}

    barrier = pltpu.get_barrier_semaphore()
    for peer in [other_core, other_chip] + [along(d) for d in others]:
        pl.semaphore_signal(barrier, inc=1, device_id=peer, device_id_type=pl.DeviceIdType.MESH)
    loads = [
        pltpu.make_async_copy(weights_hbm.at[layer], master.at[layer], load_sems.at[layer])
        for layer in range(LAYERS)
    ]
    loads.append(pltpu.make_async_copy(features_hbm, features_ref, load_sems.at[LAYERS]))
    loads.append(pltpu.make_async_copy(cotangents_hbm, cotangents_ref, load_sems.at[LAYERS + 1]))
    for load in loads:
        load.start()
    bias_all[0] = jnp.concatenate([biases_ref[...], jnp.zeros_like(biases_ref)], 0)
    pl.semaphore_wait(barrier, experts + 1)

    started = []

    def send(src, dst, sems, index, peer):
        copy = pltpu.make_async_remote_copy(
            src_ref=src,
            dst_ref=dst,
            send_sem=sems.at[(0,) + index],
            recv_sem=sems.at[(1,) + index],
            device_id=peer,
            device_id_type=pl.DeviceIdType.MESH,
        )
        copy.start()
        started.append(copy)
        return copy

    own_start = pl.multiple_of(core * 2 * SLICE + chip * SLICE, SLICE)
    half_start = pl.multiple_of(core * 2 * SLICE, 2 * SLICE)
    whole = bias_all.at[0]
    bias_copies = [
        send(whole, bias_all.at[experts - d], b_sems, (d - 1,), along(d)) for d in others
    ]
    line_copies = []
    for layer in range(LAYERS):
        loads[layer].wait()
        low[layer, 0] = master[layer].astype(jnp.bfloat16)
        line_copies.append(
            [
                send(
                    low.at[layer, 0, pl.ds(own_start, SLICE)],
                    low.at[layer, experts - d, pl.ds(own_start, SLICE)],
                    z_sems,
                    (layer, d - 1),
                    along(d),
                )
                for d in others
            ]
        )

    chip_copies = {}
    core_copies = {}

    def pass_to_chip(layer):
        chip_copies[layer] = []
        for d in others:
            line_copies[layer][experts - d - 1].wait_recv()
            part = low.at[layer, d, pl.ds(own_start, SLICE)]
            chip_copies[layer].append(send(part, part, x_sems, (layer, d - 1), other_chip))

    def pass_to_core(layer):
        core_copies[layer] = []
        for d in others:
            chip_copies[layer][d - 1].wait_recv()
            part = low.at[layer, d, pl.ds(half_start, 2 * SLICE)]
            core_copies[layer].append(send(part, part, c_sems, (layer, d - 1), other_core))

    def arrived(layer):
        for copy in core_copies[layer]:
            copy.wait_recv()

    def each_tile(body, first=0, last=tiles):
        def step(i, carry):
            body(pl.ds(pl.multiple_of(i * TILE, TILE), TILE))
            return carry

        lax.fori_loop(first, last, step, 0)

    row_of = lax.broadcasted_iota(jnp.int32, (16, rows), 0)
    position = lax.broadcasted_iota(jnp.int32, (16, rows), 1)
    named = (routes_ref[...] == (row_of + expert) % experts) & (row_of < 3 * experts)
    named = named & (position < live_ref[0])
    onehot[...] = jnp.where(named, 1.0, 0.0).astype(jnp.bfloat16)
    spread_row = lax.broadcasted_iota(jnp.int32, (16, wide), 0)
    spread_column = lax.broadcasted_iota(jnp.int32, (16, wide), 1)
    spread = jnp.where(spread_row == spread_column // width, 1.0, 0.0).astype(jnp.bfloat16)
    contract_rows = (((0,), (0,)), ((), ()))

    for copy in bias_copies:
        copy.wait_recv()
    bias_parts = []
    for layer in range(LAYERS - 1):
        whole = jnp.concatenate([bias_all[e, layer : layer + 1] for e in range(experts)], 0)
        high = whole.astype(jnp.bfloat16).astype(jnp.float32)
        middle = (whole - high).astype(jnp.bfloat16).astype(jnp.float32)
        lowest = whole - high - middle
        bias_parts.append(
            jnp.concatenate([high, middle, lowest, jnp.zeros_like(high)], 0).astype(jnp.bfloat16)
        )

    def prepare(at):
        chosen = onehot[:, at]
        mask[at, :] = lax.dot_general(
            chosen, spread, contract_rows, preferred_element_type=jnp.float32
        ).astype(jnp.bfloat16)
        for layer in range(LAYERS - 1):
            sigs[layer, at, :] = lax.dot_general(
                chosen, bias_parts[layer], contract_rows, preferred_element_type=jnp.float32
            )

    half = tiles // 2
    each_tile(prepare, 0, half)
    pass_to_chip(0)
    each_tile(prepare, half)

    def separated(block, at, slots=range(experts)):
        columns = slice(slots[0] * width, (slots[-1] + 1) * width)
        return jnp.concatenate([block] * len(slots), 1) * mask[at, columns]

    def forward(layer, first=0, last=tiles):
        def body(at):
            block = features_ref[at, :] if layer == 0 else acts[layer - 1, at, :]
            preact = (
                jnp.dot(
                    separated(block, at),
                    low[layer].reshape(wide, width),
                    preferred_element_type=jnp.float32,
                )
                + sigs[layer, at, :]
            )
            soft, sig = softplus_and_sigmoid(preact)
            acts[layer, at, :] = soft.astype(jnp.bfloat16)
            sigs[layer, at, :] = sig

        each_tile(body, first, last)

    pass_to_chip(1)
    pass_to_core(0)
    loads[LAYERS].wait()
    arrived(0)
    forward(0, 0, half)
    pass_to_chip(2)
    pass_to_core(1)
    forward(0, half)
    pass_to_chip(3)
    arrived(1)
    forward(1, 0, half)
    pass_to_core(2)
    forward(1, half)
    pass_to_core(3)
    arrived(2)
    forward(2)
    loads[LAYERS + 1].wait()

    def adjoint_of(layer, at):
        return cotangents_ref[at, :] if layer == LAYERS - 1 else adj[at, :]

    groups = (range(experts // 2, experts), range(0, experts // 2))

    def gradients(layer, slots=range(experts)):
        columns = slice(slots[0] * width, (slots[-1] + 1) * width)
        grad[:, columns] = jnp.zeros((width, len(slots) * width), jnp.float32)
        with_bias = slots[-1] == experts - 1
        if with_bias:
            bias_grad[layer] = jnp.zeros((16, width), jnp.float32)

        def body(at):
            block = adjoint_of(layer, at)
            act = features_ref[at, :] if layer == 0 else acts[layer - 1, at, :]
            grad[:, columns] += lax.dot_general(
                act, separated(block, at, slots), contract_rows, preferred_element_type=jnp.float32
            )
            if with_bias:
                bias_grad[layer] += jnp.dot(
                    onehot[:, at], block, preferred_element_type=jnp.float32
                )

        each_tile(body)

    def pull(layer, first=0, last=tiles):
        def body(at):
            parts = separated(adjoint_of(layer, at), at)
            pulled = sum(
                lax.dot_general(
                    parts[:, e * width : (e + 1) * width],
                    low[layer, e],
                    (((1,), (1,)), ((), ())),
                    preferred_element_type=jnp.float32,
                )
                for e in range(experts)
            )
            if layer > 0:
                adj[at, :] = (pulled * sigs[layer - 1, at, :]).astype(jnp.bfloat16)
            else:
                input_grads_ref[at, :] = pulled.astype(jnp.bfloat16)

        each_tile(body, first, last)

    def height(layer):
        return SLICE + (TAIL if layer == 0 else 0)

    sums = {}

    def share_core(layer, group):
        slots = groups[group]
        for e in slots:
            columns = slice(e * width, (e + 1) * width)
            if layer == 0:
                tail = jnp.concatenate(
                    [bias_grad[k, e : e + 1] for k in range(LAYERS)]
                    + [jnp.zeros((TAIL - LAYERS, width), jnp.float32)],
                    0,
                )
            for c in range(2):
                mine = pl.ds(pl.multiple_of((c * 2 + core) * SLICE, SLICE), SLICE)
                theirs = pl.ds(pl.multiple_of((c * 2 + 1 - core) * SLICE, SLICE), SLICE)
                core_keep[layer, c, e, :SLICE] = grad[mine, columns]
                core_send[layer, c, e, :SLICE] = grad[theirs, columns].astype(jnp.bfloat16)
                if layer == 0:
                    core_keep[layer, c, e, SLICE:] = tail
                    core_send[layer, c, e, SLICE:] = tail.astype(jnp.bfloat16)
        held = pl.ds(slots[0], len(slots))
        part = pl.ds(0, height(layer))
        sums["core", layer, group] = send(
            core_send.at[layer, :, held, part],
            core_recv.at[layer, :, held, part],
            core_sems,
            (layer, group),
            other_core,
        )

    def share_chip(layer, group):
        sums["core", layer, group].wait_recv()
        n = height(layer)
        slots = groups[group]
        for e in slots:
            chip_send[layer, e, :n] = (
                core_keep[layer, 1 - chip, e, :n]
                + core_recv[layer, 1 - chip, e, :n].astype(jnp.float32)
            ).astype(jnp.bfloat16)
        held = pl.ds(slots[0], len(slots))
        part = pl.ds(0, n)
        sums["chip", layer, group] = send(
            chip_send.at[layer, held, part],
            chip_recv.at[layer, held, part],
            chip_sems,
            (layer, group),
            other_chip,
        )
        for e in slots:
            chip_keep[layer, e, :n] = core_keep[layer, chip, e, :n] + core_recv[
                layer, chip, e, :n
            ].astype(jnp.float32)

    def share_line(layer, group):
        sums["chip", layer, group].wait_recv()
        n = height(layer)
        part = pl.ds(0, n)
        for d in groups[group]:
            total = chip_keep[layer, d, :n] + chip_recv[layer, d, :n].astype(jnp.float32)
            if d == 0:
                chip_keep[layer, d, :n] = total
            else:
                line_send[layer, d, :n] = total.astype(jnp.bfloat16)
                sums["line", layer, d] = send(
                    line_send.at[layer, d, part],
                    line_recv.at[layer, d - 1, part],
                    line_sems,
                    (layer, d - 1),
                    along(d),
                )

    def finish(layer):
        n = height(layer)
        total = chip_keep[layer, 0, :n]
        for d in others:
            sums["line", layer, d].wait_recv()
            total = total + line_recv[layer, d - 1, :n].astype(jnp.float32)
        share_ref[layer] = total[:SLICE]
        if layer == 0:
            bias_share_ref[...] = total[SLICE : SLICE + 2 * LAYERS]

    gradients(3)
    share_core(3, 0)
    share_core(3, 1)
    arrived(3)
    pull(3)
    share_chip(3, 0)
    share_chip(3, 1)
    gradients(2)
    share_core(2, 0)
    share_core(2, 1)
    share_line(3, 0)
    share_line(3, 1)
    pull(2)
    share_chip(2, 0)
    share_chip(2, 1)
    gradients(1)
    share_core(1, 0)
    share_core(1, 1)
    share_line(2, 0)
    share_line(2, 1)
    pull(1)
    share_chip(1, 0)
    share_chip(1, 1)
    gradients(0, groups[0])
    share_core(0, 0)
    gradients(0, groups[1])
    share_core(0, 1)
    share_chip(0, 0)
    share_line(1, 0)
    share_line(1, 1)
    pull(0, 0, half)
    share_chip(0, 1)
    share_line(0, 0)
    pull(0, half)
    finish(3)
    share_line(0, 1)
    finish(2)
    finish(1)
    finish(0)
    for copy in started:
        copy.wait_send()


def adam_kernel(
    grads_hbm,
    weights_hbm,
    biases_ref,
    share_ref,
    bias_share_ref,
    first_ref,
    second_ref,
    bias_first_ref,
    bias_second_ref,
    input_grads_hbm,
    new_weights_ref,
    new_first_ref,
    new_second_ref,
    new_biases_ref,
    new_bias_first_ref,
    new_bias_second_ref,
    master,
    sems,
):
    replica = lax.axis_index("replica")
    width = biases_ref.shape[1]
    rows = pl.ds(pl.multiple_of(replica * SLICE, SLICE), SLICE)
    fetch = pltpu.make_async_copy(weights_hbm.at[:, rows], master, sems.at[0])
    fetch.start()
    moved = pltpu.make_async_copy(grads_hbm, input_grads_hbm, sems.at[1])
    moved.start()

    def own_columns(block):
        picked = block[:, :SLICE]
        for k in range(1, width // SLICE):
            picked = jnp.where(replica == k, block[:, k * SLICE : (k + 1) * SLICE], picked)
        return picked

    updated, one, two = adam_update(
        own_columns(biases_ref[...]),
        bias_first_ref[...],
        bias_second_ref[...],
        own_columns(bias_share_ref[:LAYERS]),
    )
    new_biases_ref[...] = updated
    new_bias_first_ref[...] = one
    new_bias_second_ref[...] = two
    fetch.wait()
    for layer in range(LAYERS):
        updated, one, two = adam_update(
            master[layer], first_ref[layer], second_ref[layer], share_ref[layer]
        )
        new_weights_ref[layer] = updated
        new_first_ref[layer] = one
        new_second_ref[layer] = two
    moved.wait()


def fused_shards(
    features,
    cotangents,
    routes,
    live_counts,
    weights,
    biases,
    first_moment,
    second_moment,
    bias_first,
    bias_second,
):
    experts = lax.axis_size("expert")
    rows, width = features.shape
    wide = experts * width
    tall = SLICE + TAIL
    f32, bf16 = jnp.float32, jnp.bfloat16
    vmem = pl.BlockSpec(memory_space=pltpu.VMEM)
    moment = jax.ShapeDtypeStruct(first_moment.shape[1:], f32)
    bias_moment = jax.ShapeDtypeStruct(bias_first.shape[1:], f32)
    anywhere = pl.BlockSpec(memory_space=pl.ANY)
    grads, share, bias_share = pl.pallas_call(
        functools.partial(fused_kernel, experts),
        out_shape=(
            jax.ShapeDtypeStruct((rows, width), bf16),
            moment,
            jax.ShapeDtypeStruct((2 * LAYERS, width), f32),
        ),
        in_specs=[
            pl.BlockSpec(memory_space=pltpu.SMEM),
            anywhere,
            anywhere,
            vmem,
            anywhere,
            vmem,
        ],
        out_specs=(vmem,) * 3,
        scratch_shapes=[
            pltpu.VMEM((LAYERS, width, width), f32),
            pltpu.VMEM((rows, width), bf16),
            pltpu.VMEM((rows, width), bf16),
            pltpu.VMEM((LAYERS, experts, width, width), bf16),
            pltpu.VMEM((experts, 2 * LAYERS, width), f32),
            pltpu.VMEM((16, rows), bf16),
            pltpu.VMEM((rows, wide), bf16),
            pltpu.VMEM((LAYERS - 1, rows, width), bf16),
            pltpu.VMEM((LAYERS - 1, rows, width), f32),
            pltpu.VMEM((rows, width), bf16),
            pltpu.VMEM((width, wide), f32),
            pltpu.VMEM((LAYERS, 16, width), f32),
            pltpu.VMEM((LAYERS, 2, experts, tall, width), bf16),
            pltpu.VMEM((LAYERS, 2, experts, tall, width), bf16),
            pltpu.VMEM((LAYERS, 2, experts, tall, width), f32),
            pltpu.VMEM((LAYERS, experts, tall, width), bf16),
            pltpu.VMEM((LAYERS, experts, tall, width), bf16),
            pltpu.VMEM((LAYERS, experts, tall, width), f32),
            pltpu.VMEM((LAYERS, experts, tall, width), bf16),
            pltpu.VMEM((LAYERS, experts - 1, tall, width), bf16),
            pltpu.SemaphoreType.DMA((2, LAYERS, experts - 1)),
            pltpu.SemaphoreType.DMA((2, LAYERS, experts - 1)),
            pltpu.SemaphoreType.DMA((2, LAYERS, experts - 1)),
            pltpu.SemaphoreType.DMA((2, experts - 1)),
            pltpu.SemaphoreType.DMA((2, LAYERS, 2)),
            pltpu.SemaphoreType.DMA((2, LAYERS, 2)),
            pltpu.SemaphoreType.DMA((2, LAYERS, experts - 1)),
            pltpu.SemaphoreType.DMA((LAYERS + 2,)),
        ],
        compiler_params=pltpu.CompilerParams(
            collective_id=0, has_side_effects=True, vmem_limit_bytes=56 * 1024 * 1024
        ),
        cost_estimate=pl.CostEstimate(
            flops=22 * rows * wide * width, bytes_accessed=6 * 2**20, transcendentals=9 * rows * width
        ),
    )(
        live_counts,
        features,
        cotangents,
        routes.reshape(1, rows),
        weights[0],
        biases[0],
    )
    outs = pl.pallas_call(
        adam_kernel,
        out_shape=(
            jax.ShapeDtypeStruct((rows, width), bf16),
            moment,
            moment,
            moment,
            bias_moment,
            bias_moment,
            bias_moment,
        ),
        in_specs=[anywhere, anywhere] + [vmem] * 7,
        out_specs=(anywhere,) + (vmem,) * 6,
        scratch_shapes=[
            pltpu.VMEM((LAYERS, SLICE, width), f32),
            pltpu.SemaphoreType.DMA((2,)),
        ],
    )(
        grads,
        weights[0],
        biases[0],
        share,
        bias_share,
        first_moment[0],
        second_moment[0],
        bias_first[0],
        bias_second[0],
    )
    return (outs[0],) + tuple(out[None] for out in outs[1:])


def shards(*arrays):
    if lax.axis_size("expert") == 4 and lax.axis_size("replica") == 4:
        return fused_shards(*arrays)
    return routed_shards(*arrays)


def solution(mesh):
    return jax.shard_map(
        shards,
        mesh=mesh,
        in_specs=(
            P(("groups", "expert", "replica"), None),
            P(("groups", "expert", "replica"), None),
            P(("groups", "expert", "replica"), None),
            P(("groups", "expert", "replica")),
            P(("groups", "expert"), None, None, None),
            P(("groups", "expert"), None, None),
            P(("groups", "expert"), None, "replica", None),
            P(("groups", "expert"), None, "replica", None),
            P(("groups", "expert"), None, "replica"),
            P(("groups", "expert"), None, "replica"),
        ),
        out_specs=(
            P(("groups", "expert", "replica"), None),
            P(("groups", "expert"), None, "replica", None),
            P(("groups", "expert"), None, "replica", None),
            P(("groups", "expert"), None, "replica", None),
            P(("groups", "expert"), None, "replica"),
            P(("groups", "expert"), None, "replica"),
            P(("groups", "expert"), None, "replica"),
        ),
        check_vma=False,
    )
```

```python
import functools
import math

import jax
import jax.numpy as jnp
from jax import lax
from jax.experimental import pallas as pl
from jax.experimental.pallas import tpu as pltpu
from jax.sharding import PartitionSpec as P

LAYERS = 4
ROWS_DEV = 2048


beta_first = 0.9
beta_second = 0.999
learn_rate = 0.05
adam_epsilon = 1e-08
first_fix = 1.0 - 0.9**10
second_fix = 1.0 - 0.999**10


def forward_layers(weights_low, bias_rows, inputs_rows):
    activations = [inputs_rows]
    preacts = []
    for layer in range(LAYERS - 1):
        preact = (
            jnp.dot(activations[-1], weights_low[layer], preferred_element_type=jnp.float32)
            + bias_rows[layer]
        )
        preacts.append(preact)
        activations.append(jax.nn.softplus(preact).astype(jnp.bfloat16))
    return (activations, preacts)


def adjoint_chain(weights_low, preacts, adjoint):
    adjoints = [None] * LAYERS
    input_grad = None
    for layer in reversed(range(LAYERS)):
        adjoints[layer] = adjoint
        pulled = lax.dot_general(
            adjoint,
            weights_low[layer],
            (((1,), (1,)), ((), ())),
            preferred_element_type=jnp.float32,
        )
        if layer > 0:
            adjoint = (pulled * jax.nn.sigmoid(preacts[layer - 1])).astype(jnp.bfloat16)
        else:
            input_grad = pulled.astype(jnp.bfloat16)
    return (adjoints, input_grad)


def gradient_terms(activations, adjoints):
    weight_grads = []
    bias_grads = []
    for layer in range(LAYERS):
        weight_grads.append(
            lax.dot_general(
                activations[layer],
                adjoints[layer],
                (((0,), (0,)), ((), ())),
                preferred_element_type=jnp.float32,
            )
        )
        bias_grads.append(jnp.sum(adjoints[layer].astype(jnp.float32), 0))
    return (jnp.stack(weight_grads)[None], jnp.stack(bias_grads)[None])


def adam_update(master, moment_one, moment_two, gradient):
    scaled = gradient / math.sqrt(ROWS_DEV)
    moment_one = beta_first * moment_one + (1.0 - beta_first) * scaled
    moment_two = beta_second * moment_two + (1.0 - beta_second) * scaled * scaled
    updated = master - learn_rate * (moment_one / first_fix) / (
        jnp.sqrt(moment_two / second_fix) + adam_epsilon
    )
    return (updated, moment_one, moment_two)


def routed_shards(
    features,
    cotangents,
    routes,
    live_counts,
    weights,
    biases,
    first_moment,
    second_moment,
    bias_first,
    bias_second,
):
    expert_count = lax.axis_size("expert")
    replicas = lax.axis_size("replica")
    rows_here = features.shape[0]
    feature_width = features.shape[1]
    capacity = 2 * rows_here // expert_count
    route_ids = routes[:, 0]
    positions = lax.iota(jnp.int32, rows_here)
    is_live = positions < live_counts[0]
    masked = jnp.where(is_live[:, None], cotangents, jnp.zeros_like(cotangents))
    onehot = (route_ids[:, None] == lax.iota(jnp.int32, expert_count)[None, :]).astype(jnp.int32)
    weights_low = weights[0].astype(jnp.bfloat16)
    dump_slot = expert_count * capacity
    slot_rank = jnp.sum((jnp.cumsum(onehot, 0) - onehot) * onehot, 1)
    slot_index = route_ids * capacity + slot_rank

    def place(row_data):
        buffer = (
            jnp.zeros((expert_count * capacity, feature_width), row_data.dtype)
            .at[slot_index]
            .set(row_data, mode="drop")
        )
        return buffer.reshape(expert_count, capacity, feature_width)

    got_rows, got_adjoint = (
        lax.all_to_all(place(features), "expert", split_axis=0, concat_axis=0, tiled=True),
        lax.all_to_all(place(masked), "expert", split_axis=0, concat_axis=0, tiled=True),
    )
    inputs_rows = got_rows.reshape(-1, feature_width)
    adjoint = got_adjoint.reshape(-1, feature_width)
    activations, preacts = forward_layers(weights_low, biases[0], inputs_rows)
    adjoints, input_grad = adjoint_chain(weights_low, preacts, adjoint)
    weight_grads, bias_grads = gradient_terms(activations, adjoints)
    returned = lax.all_to_all(
        input_grad.reshape(expert_count, capacity, feature_width),
        "expert",
        split_axis=0,
        concat_axis=0,
        tiled=True,
    )
    flat = returned.reshape(-1, feature_width)
    picked = flat[jnp.minimum(slot_index, dump_slot - 1)]
    input_grads = jnp.where((slot_index < dump_slot)[:, None], picked, jnp.zeros_like(picked))
    shard_rows = feature_width // replicas
    shard_start = lax.axis_index("replica") * shard_rows
    weight_share, bias_share = (
        lax.psum_scatter(
            weight_grads.astype(jnp.bfloat16), "replica", scatter_dimension=2, tiled=True
        ).astype(jnp.float32),
        lax.psum_scatter(
            bias_grads.astype(jnp.bfloat16), "replica", scatter_dimension=2, tiled=True
        ).astype(jnp.float32),
    )
    master_weights = lax.dynamic_slice_in_dim(weights, shard_start, shard_rows, 2)
    master_biases = lax.dynamic_slice_in_dim(biases, shard_start, shard_rows, 2)
    new_weights, new_first, new_second = adam_update(
        master_weights, first_moment, second_moment, weight_share
    )
    new_biases, new_bias_first, new_bias_second = adam_update(
        master_biases, bias_first, bias_second, bias_share
    )
    return (
        input_grads,
        new_weights,
        new_first,
        new_second,
        new_biases,
        new_bias_first,
        new_bias_second,
    )


TILE = 1024
SLICE = 64
CHUNKS = LAYERS
TAIL = 16


def softplus_and_sigmoid(x):
    small = jnp.exp(-jnp.abs(x))
    total = 1.0 + small
    inverse = pl.reciprocal(total)
    log_part = jnp.where(small < 1e-3, small - 0.5 * small * small, jnp.log(total))
    return jnp.maximum(x, 0.0) + log_part, jnp.where(x >= 0.0, inverse, small * inverse)


def fused_kernel(
    experts,
    live_ref,
    features_hbm,
    cotangents_hbm,
    routes_ref,
    weights_hbm,
    biases_ref,
    input_grads_ref,
    share_ref,
    bias_share_ref,
    master,
    features_ref,
    cotangents_ref,
    low,
    bias_all,
    onehot,
    mask,
    acts,
    sigs,
    adj,
    grad,
    bias_grad,
    core_send,
    core_recv,
    core_keep,
    chip_send,
    chip_recv,
    chip_keep,
    line_send,
    line_recv,
    z_sems,
    x_sems,
    c_sems,
    b_sems,
    core_sems,
    chip_sems,
    line_sems,
    load_sems,
):
    rows, width = features_ref.shape
    wide = experts * width
    tiles = rows // TILE
    expert = lax.axis_index("expert")
    replica = lax.axis_index("replica")
    chip, core = replica // 2, replica % 2
    other_core = {"replica": chip * 2 + 1 - core}
    other_chip = {"replica": (1 - chip) * 2 + core}
    others = range(1, experts)

    def along(d):
        return {"expert": lax.rem(expert + d, experts)}

    barrier = pltpu.get_barrier_semaphore()
    for peer in [other_core, other_chip] + [along(d) for d in others]:
        pl.semaphore_signal(barrier, inc=1, device_id=peer, device_id_type=pl.DeviceIdType.MESH)
    loads = [
        pltpu.make_async_copy(weights_hbm.at[layer], master.at[layer], load_sems.at[layer])
        for layer in range(LAYERS)
    ]
    loads.append(pltpu.make_async_copy(features_hbm, features_ref, load_sems.at[LAYERS]))
    loads.append(pltpu.make_async_copy(cotangents_hbm, cotangents_ref, load_sems.at[LAYERS + 1]))
    for load in loads:
        load.start()
    bias_all[0] = jnp.concatenate([biases_ref[...], jnp.zeros_like(biases_ref)], 0)
    pl.semaphore_wait(barrier, experts + 1)

    started = []

    def send(src, dst, sems, index, peer):
        copy = pltpu.make_async_remote_copy(
            src_ref=src,
            dst_ref=dst,
            send_sem=sems.at[(0,) + index],
            recv_sem=sems.at[(1,) + index],
            device_id=peer,
            device_id_type=pl.DeviceIdType.MESH,
        )
        copy.start()
        started.append(copy)
        return copy

    own_start = pl.multiple_of(core * 2 * SLICE + chip * SLICE, SLICE)
    half_start = pl.multiple_of(core * 2 * SLICE, 2 * SLICE)
    whole = bias_all.at[0]
    bias_copies = [
        send(whole, bias_all.at[experts - d], b_sems, (d - 1,), along(d)) for d in others
    ]
    line_copies = []
    for layer in range(LAYERS):
        loads[layer].wait()
        low[layer, 0] = master[layer].astype(jnp.bfloat16)
        line_copies.append(
            [
                send(
                    low.at[layer, 0, pl.ds(own_start, SLICE)],
                    low.at[layer, experts - d, pl.ds(own_start, SLICE)],
                    z_sems,
                    (layer, d - 1),
                    along(d),
                )
                for d in others
            ]
        )

    chip_copies = {}
    core_copies = {}

    def pass_to_chip(layer):
        chip_copies[layer] = []
        for d in others:
            line_copies[layer][experts - d - 1].wait_recv()
            part = low.at[layer, d, pl.ds(own_start, SLICE)]
            chip_copies[layer].append(send(part, part, x_sems, (layer, d - 1), other_chip))

    def pass_to_core(layer):
        core_copies[layer] = []
        for d in others:
            chip_copies[layer][d - 1].wait_recv()
            part = low.at[layer, d, pl.ds(half_start, 2 * SLICE)]
            core_copies[layer].append(send(part, part, c_sems, (layer, d - 1), other_core))

    def arrived(layer):
        for copy in core_copies[layer]:
            copy.wait_recv()

    def each_tile(body, first=0, last=tiles):
        def step(i, carry):
            body(pl.ds(pl.multiple_of(i * TILE, TILE), TILE))
            return carry

        lax.fori_loop(first, last, step, 0)

    row_of = lax.broadcasted_iota(jnp.int32, (16, rows), 0)
    position = lax.broadcasted_iota(jnp.int32, (16, rows), 1)
    named = (routes_ref[...] == (row_of + expert) % experts) & (row_of < 3 * experts)
    named = named & (position < live_ref[0])
    onehot[...] = jnp.where(named, 1.0, 0.0).astype(jnp.bfloat16)
    spread_row = lax.broadcasted_iota(jnp.int32, (16, wide), 0)
    spread_column = lax.broadcasted_iota(jnp.int32, (16, wide), 1)
    spread = jnp.where(spread_row == spread_column // width, 1.0, 0.0).astype(jnp.bfloat16)
    contract_rows = (((0,), (0,)), ((), ()))

    for copy in bias_copies:
        copy.wait_recv()
    bias_parts = []
    for layer in range(LAYERS - 1):
        whole = jnp.concatenate([bias_all[e, layer : layer + 1] for e in range(experts)], 0)
        high = whole.astype(jnp.bfloat16).astype(jnp.float32)
        middle = (whole - high).astype(jnp.bfloat16).astype(jnp.float32)
        lowest = whole - high - middle
        bias_parts.append(
            jnp.concatenate([high, middle, lowest, jnp.zeros_like(high)], 0).astype(jnp.bfloat16)
        )

    def prepare(at):
        chosen = onehot[:, at]
        mask[at, :] = lax.dot_general(
            chosen, spread, contract_rows, preferred_element_type=jnp.float32
        ).astype(jnp.bfloat16)
        for layer in range(LAYERS - 1):
            sigs[layer, at, :] = lax.dot_general(
                chosen, bias_parts[layer], contract_rows, preferred_element_type=jnp.float32
            )

    half = tiles // 2
    each_tile(prepare, 0, half)
    pass_to_chip(0)
    each_tile(prepare, half)

    def separated(block, at, slots=range(experts)):
        columns = slice(slots[0] * width, (slots[-1] + 1) * width)
        return jnp.concatenate([block] * len(slots), 1) * mask[at, columns]

    def forward(layer, first=0, last=tiles):
        def body(at):
            block = features_ref[at, :] if layer == 0 else acts[layer - 1, at, :]
            preact = (
                jnp.dot(
                    separated(block, at),
                    low[layer].reshape(wide, width),
                    preferred_element_type=jnp.float32,
                )
                + sigs[layer, at, :]
            )
            soft, sig = softplus_and_sigmoid(preact)
            acts[layer, at, :] = soft.astype(jnp.bfloat16)
            sigs[layer, at, :] = sig

        each_tile(body, first, last)

    pass_to_chip(1)
    pass_to_core(0)
    loads[LAYERS].wait()
    arrived(0)
    forward(0, 0, half)
    pass_to_chip(2)
    pass_to_core(1)
    forward(0, half)
    pass_to_chip(3)
    arrived(1)
    forward(1, 0, half)
    pass_to_core(2)
    forward(1, half)
    pass_to_core(3)
    arrived(2)
    forward(2)
    loads[LAYERS + 1].wait()

    def adjoint_of(layer, at):
        return cotangents_ref[at, :] if layer == LAYERS - 1 else adj[at, :]

    groups = (range(experts // 2, experts), range(0, experts // 2))

    def gradients(layer, slots=range(experts)):
        columns = slice(slots[0] * width, (slots[-1] + 1) * width)
        grad[:, columns] = jnp.zeros((width, len(slots) * width), jnp.float32)
        with_bias = slots[-1] == experts - 1
        if with_bias:
            bias_grad[layer] = jnp.zeros((16, width), jnp.float32)

        def body(at):
            block = adjoint_of(layer, at)
            act = features_ref[at, :] if layer == 0 else acts[layer - 1, at, :]
            grad[:, columns] += lax.dot_general(
                act, separated(block, at, slots), contract_rows, preferred_element_type=jnp.float32
            )
            if with_bias:
                bias_grad[layer] += jnp.dot(
                    onehot[:, at], block, preferred_element_type=jnp.float32
                )

        each_tile(body)

    def pull(layer, first=0, last=tiles):
        def body(at):
            parts = separated(adjoint_of(layer, at), at)
            pulled = sum(
                lax.dot_general(
                    parts[:, e * width : (e + 1) * width],
                    low[layer, e],
                    (((1,), (1,)), ((), ())),
                    preferred_element_type=jnp.float32,
                )
                for e in range(experts)
            )
            if layer > 0:
                adj[at, :] = (pulled * sigs[layer - 1, at, :]).astype(jnp.bfloat16)
            else:
                input_grads_ref[at, :] = pulled.astype(jnp.bfloat16)

        each_tile(body, first, last)

    def height(layer):
        return SLICE + (TAIL if layer == 0 else 0)

    sums = {}

    def share_core(layer, group):
        slots = groups[group]
        for e in slots:
            columns = slice(e * width, (e + 1) * width)
            if layer == 0:
                tail = jnp.concatenate(
                    [bias_grad[k, e : e + 1] for k in range(LAYERS)]
                    + [jnp.zeros((TAIL - LAYERS, width), jnp.float32)],
                    0,
                )
            for c in range(2):
                mine = pl.ds(pl.multiple_of((c * 2 + core) * SLICE, SLICE), SLICE)
                theirs = pl.ds(pl.multiple_of((c * 2 + 1 - core) * SLICE, SLICE), SLICE)
                core_keep[layer, c, e, :SLICE] = grad[mine, columns]
                core_send[layer, c, e, :SLICE] = grad[theirs, columns].astype(jnp.bfloat16)
                if layer == 0:
                    core_keep[layer, c, e, SLICE:] = tail
                    core_send[layer, c, e, SLICE:] = tail.astype(jnp.bfloat16)
        held = pl.ds(slots[0], len(slots))
        part = pl.ds(0, height(layer))
        sums["core", layer, group] = send(
            core_send.at[layer, :, held, part],
            core_recv.at[layer, :, held, part],
            core_sems,
            (layer, group),
            other_core,
        )

    def share_chip(layer, group):
        sums["core", layer, group].wait_recv()
        n = height(layer)
        slots = groups[group]
        for e in slots:
            chip_send[layer, e, :n] = (
                core_keep[layer, 1 - chip, e, :n]
                + core_recv[layer, 1 - chip, e, :n].astype(jnp.float32)
            ).astype(jnp.bfloat16)
        held = pl.ds(slots[0], len(slots))
        part = pl.ds(0, n)
        sums["chip", layer, group] = send(
            chip_send.at[layer, held, part],
            chip_recv.at[layer, held, part],
            chip_sems,
            (layer, group),
            other_chip,
        )
        for e in slots:
            chip_keep[layer, e, :n] = core_keep[layer, chip, e, :n] + core_recv[
                layer, chip, e, :n
            ].astype(jnp.float32)

    def share_line(layer, group):
        sums["chip", layer, group].wait_recv()
        n = height(layer)
        part = pl.ds(0, n)
        for d in groups[group]:
            total = chip_keep[layer, d, :n] + chip_recv[layer, d, :n].astype(jnp.float32)
            if d == 0:
                chip_keep[layer, d, :n] = total
            else:
                line_send[layer, d, :n] = total.astype(jnp.bfloat16)
                sums["line", layer, d] = send(
                    line_send.at[layer, d, part],
                    line_recv.at[layer, d - 1, part],
                    line_sems,
                    (layer, d - 1),
                    along(d),
                )

    def finish(layer):
        n = height(layer)
        total = chip_keep[layer, 0, :n]
        for d in others:
            sums["line", layer, d].wait_recv()
            total = total + line_recv[layer, d - 1, :n].astype(jnp.float32)
        share_ref[layer] = total[:SLICE]
        if layer == 0:
            bias_share_ref[...] = total[SLICE : SLICE + 2 * LAYERS]

    gradients(3)
    share_core(3, 0)
    share_core(3, 1)
    arrived(3)
    pull(3)
    share_chip(3, 0)
    share_chip(3, 1)
    gradients(2)
    share_core(2, 0)
    share_core(2, 1)
    share_line(3, 0)
    share_line(3, 1)
    pull(2)
    share_chip(2, 0)
    share_chip(2, 1)
    gradients(1)
    share_core(1, 0)
    share_core(1, 1)
    share_line(2, 0)
    share_line(2, 1)
    pull(1)
    share_chip(1, 0)
    share_chip(1, 1)
    gradients(0, groups[0])
    share_core(0, 0)
    gradients(0, groups[1])
    share_core(0, 1)
    share_chip(0, 0)
    share_line(1, 0)
    share_line(1, 1)
    pull(0, 0, half)
    share_chip(0, 1)
    share_line(0, 0)
    pull(0, half)
    finish(3)
    share_line(0, 1)
    finish(2)
    finish(1)
    finish(0)
    for copy in started:
        copy.wait_send()


def adam_kernel(
    grads_hbm,
    weights_hbm,
    biases_ref,
    share_ref,
    bias_share_ref,
    first_ref,
    second_ref,
    bias_first_ref,
    bias_second_ref,
    input_grads_hbm,
    new_weights_ref,
    new_first_ref,
    new_second_ref,
    new_biases_ref,
    new_bias_first_ref,
    new_bias_second_ref,
    master,
    passing,
    sems,
):
    replica = lax.axis_index("replica")
    width = biases_ref.shape[1]
    rows = pl.ds(pl.multiple_of(replica * SLICE, SLICE), SLICE)
    fetch = pltpu.make_async_copy(weights_hbm.at[:, rows], master, sems.at[0])
    fetch.start()
    chunk = grads_hbm.shape[0] // CHUNKS
    parts = [pl.ds(k * chunk, chunk) for k in range(CHUNKS)]
    inward = [
        pltpu.make_async_copy(grads_hbm.at[part], passing.at[part], sems.at[1 + k])
        for k, part in enumerate(parts)
    ]
    outward = [
        pltpu.make_async_copy(passing.at[part], input_grads_hbm.at[part], sems.at[1 + CHUNKS + k])
        for k, part in enumerate(parts)
    ]
    for copy in inward:
        copy.start()

    def own_columns(block):
        picked = block[:, :SLICE]
        for k in range(1, width // SLICE):
            picked = jnp.where(replica == k, block[:, k * SLICE : (k + 1) * SLICE], picked)
        return picked

    updated, one, two = adam_update(
        own_columns(biases_ref[...]),
        bias_first_ref[...],
        bias_second_ref[...],
        own_columns(bias_share_ref[:LAYERS]),
    )
    new_biases_ref[...] = updated
    new_bias_first_ref[...] = one
    new_bias_second_ref[...] = two
    fetch.wait()
    for layer in range(LAYERS):
        updated, one, two = adam_update(
            master[layer], first_ref[layer], second_ref[layer], share_ref[layer]
        )
        new_weights_ref[layer] = updated
        new_first_ref[layer] = one
        new_second_ref[layer] = two
        inward[layer].wait()
        outward[layer].start()
    for copy in outward:
        copy.wait()


def fused_shards(
    features,
    cotangents,
    routes,
    live_counts,
    weights,
    biases,
    first_moment,
    second_moment,
    bias_first,
    bias_second,
):
    experts = lax.axis_size("expert")
    rows, width = features.shape
    wide = experts * width
    tall = SLICE + TAIL
    f32, bf16 = jnp.float32, jnp.bfloat16
    vmem = pl.BlockSpec(memory_space=pltpu.VMEM)
    moment = jax.ShapeDtypeStruct(first_moment.shape[1:], f32)
    bias_moment = jax.ShapeDtypeStruct(bias_first.shape[1:], f32)
    anywhere = pl.BlockSpec(memory_space=pl.ANY)
    grads, share, bias_share = pl.pallas_call(
        functools.partial(fused_kernel, experts),
        out_shape=(
            jax.ShapeDtypeStruct((rows, width), bf16),
            moment,
            jax.ShapeDtypeStruct((2 * LAYERS, width), f32),
        ),
        in_specs=[
            pl.BlockSpec(memory_space=pltpu.SMEM),
            anywhere,
            anywhere,
            vmem,
            anywhere,
            vmem,
        ],
        out_specs=(vmem,) * 3,
        scratch_shapes=[
            pltpu.VMEM((LAYERS, width, width), f32),
            pltpu.VMEM((rows, width), bf16),
            pltpu.VMEM((rows, width), bf16),
            pltpu.VMEM((LAYERS, experts, width, width), bf16),
            pltpu.VMEM((experts, 2 * LAYERS, width), f32),
            pltpu.VMEM((16, rows), bf16),
            pltpu.VMEM((rows, wide), bf16),
            pltpu.VMEM((LAYERS - 1, rows, width), bf16),
            pltpu.VMEM((LAYERS - 1, rows, width), f32),
            pltpu.VMEM((rows, width), bf16),
            pltpu.VMEM((width, wide), f32),
            pltpu.VMEM((LAYERS, 16, width), f32),
            pltpu.VMEM((LAYERS, 2, experts, tall, width), bf16),
            pltpu.VMEM((LAYERS, 2, experts, tall, width), bf16),
            pltpu.VMEM((LAYERS, 2, experts, tall, width), f32),
            pltpu.VMEM((LAYERS, experts, tall, width), bf16),
            pltpu.VMEM((LAYERS, experts, tall, width), bf16),
            pltpu.VMEM((LAYERS, experts, tall, width), f32),
            pltpu.VMEM((LAYERS, experts, tall, width), bf16),
            pltpu.VMEM((LAYERS, experts - 1, tall, width), bf16),
            pltpu.SemaphoreType.DMA((2, LAYERS, experts - 1)),
            pltpu.SemaphoreType.DMA((2, LAYERS, experts - 1)),
            pltpu.SemaphoreType.DMA((2, LAYERS, experts - 1)),
            pltpu.SemaphoreType.DMA((2, experts - 1)),
            pltpu.SemaphoreType.DMA((2, LAYERS, 2)),
            pltpu.SemaphoreType.DMA((2, LAYERS, 2)),
            pltpu.SemaphoreType.DMA((2, LAYERS, experts - 1)),
            pltpu.SemaphoreType.DMA((LAYERS + 2,)),
        ],
        compiler_params=pltpu.CompilerParams(
            collective_id=0, has_side_effects=True, vmem_limit_bytes=56 * 1024 * 1024
        ),
        cost_estimate=pl.CostEstimate(
            flops=22 * rows * wide * width, bytes_accessed=6 * 2**20, transcendentals=9 * rows * width
        ),
    )(
        live_counts,
        features,
        cotangents,
        routes.reshape(1, rows),
        weights[0],
        biases[0],
    )
    outs = pl.pallas_call(
        adam_kernel,
        out_shape=(
            jax.ShapeDtypeStruct((rows, width), bf16),
            moment,
            moment,
            moment,
            bias_moment,
            bias_moment,
            bias_moment,
        ),
        in_specs=[anywhere, anywhere] + [vmem] * 7,
        out_specs=(anywhere,) + (vmem,) * 6,
        scratch_shapes=[
            pltpu.VMEM((LAYERS, SLICE, width), f32),
            pltpu.VMEM((rows, width), bf16),
            pltpu.SemaphoreType.DMA((1 + 2 * CHUNKS,)),
        ],
    )(
        grads,
        weights[0],
        biases[0],
        share,
        bias_share,
        first_moment[0],
        second_moment[0],
        bias_first[0],
        bias_second[0],
    )
    return (outs[0],) + tuple(out[None] for out in outs[1:])


def shards(*arrays):
    if lax.axis_size("expert") == 4 and lax.axis_size("replica") == 4:
        return fused_shards(*arrays)
    return routed_shards(*arrays)


def solution(mesh):
    return jax.shard_map(
        shards,
        mesh=mesh,
        in_specs=(
            P(("groups", "expert", "replica"), None),
            P(("groups", "expert", "replica"), None),
            P(("groups", "expert", "replica"), None),
            P(("groups", "expert", "replica")),
            P(("groups", "expert"), None, None, None),
            P(("groups", "expert"), None, None),
            P(("groups", "expert"), None, "replica", None),
            P(("groups", "expert"), None, "replica", None),
            P(("groups", "expert"), None, "replica"),
            P(("groups", "expert"), None, "replica"),
        ),
        out_specs=(
            P(("groups", "expert", "replica"), None),
            P(("groups", "expert"), None, "replica", None),
            P(("groups", "expert"), None, "replica", None),
            P(("groups", "expert"), None, "replica", None),
            P(("groups", "expert"), None, "replica"),
            P(("groups", "expert"), None, "replica"),
            P(("groups", "expert"), None, "replica"),
        ),
        check_vma=False,
    )
```
